128 devices in a mesh: occ: 64 (over z, y, x), aux: 2 (over core).
Axes of the slice: x: 4, y: 4, z: 4, core: 2. Of those that a mesh axis runs over, the one named last changes fastest.
Arguments:
- ints: bfloat16 [64, 1024, 4096], P('occ', None, 'aux'), may hold values from -0.75 to 0.75
- occ_energy: float32 [64, 4], P('occ'), may hold values from -2 to -0.5
- vir_energy: float32 [64, 256], P('occ'), may hold values from 0.5 to 4
- partners: int32 [64, 2], P('occ'), may hold values from -1 to 63, as said below
Outputs:
- gamma: float32 [64, 1024, 4096], P('occ', None, 'aux')
The draws below stay inside these ranges and needn't reach their ends.
Inputs may be any that keep to these rules, and one draw needn't show every extreme that they name: partners[I, k] is -1 or a block J with I < J <= I + 2; the entries of one row differ when not -1.
All inputs are finite; a program needn't handle non-finite values.
Results may differ from the reference program's by a relative error of at most 0.012.
Values may be sent and summed in bfloat16 or wider, within the bound.
A program may use at most 128 MiB of HBM per device.

```python
import jax
import jax.numpy as jnp
from jax import lax

ORBS = 4
VIRT = 256
AUX = 4096
REACH = 2
BLOCKS = 64
PAIR_ROWS = 1024


def draw_partners(key, part):
    key = jax.random.fold_in(key, 7)
    first_key, second_key = jax.random.split(key)
    flipped = jax.random.randint(first_key, (BLOCKS, 1), 0, 2)
    offsets = jnp.arange(1, REACH + 1, dtype=jnp.int32)[None, :]
    offsets = jnp.where(flipped == 1, REACH + 1 - offsets, offsets)
    live = jax.random.randint(second_key, (BLOCKS, REACH), 0, 4) > 0
    blocks_here = jnp.arange(BLOCKS, dtype=jnp.int32)[:, None]
    live = live | (blocks_here == BLOCKS - REACH)
    target = blocks_here + offsets
    return jnp.where(live & (target < BLOCKS), target, -1).astype(jnp.int32)


def steps_of(key, dims, cuts, least, high):
    factor_of = 1.0
    for dim, parts in cuts:
        steps = jax.random.uniform(jax.random.fold_in(jax.random.fold_in(key, 6), dim), (parts,), jnp.float32, least / len(cuts), high / len(cuts))
        factor_of = factor_of * jnp.repeat(jnp.exp(steps), dims[dim] // parts).reshape((-1,) + (1,) * (len(dims) - 1 - dim))
    return factor_of


def centred(own_key, dims, width, reach, cuts=(), kind=jnp.bfloat16):
    drawn = width * jax.random.normal(own_key, dims, jnp.float32)
    if cuts:
        drawn = drawn * steps_of(own_key, dims, cuts, -0.22, 0.18)
    return jnp.clip(drawn, -reach, reach).astype(kind)


def setup_inputs(seed: int = 0) -> dict:
    keys = jax.random.split(jax.random.key(seed), 5)
    ints = centred(keys[0], (BLOCKS, PAIR_ROWS, AUX), (AUX ** -0.25), 0.75, ((0, 64), (2, 2)))
    occ_energy = jnp.clip(-2.0 + 1.5 * jax.random.uniform(keys[1], (BLOCKS, ORBS), jnp.float32) ** steps_of(keys[1], (BLOCKS, ORBS), ((0, 64),), -0.2, 0.2), -2.0, -0.5)
    vir_energy = jnp.clip(0.5 + 3.5 * jax.random.uniform(keys[2], (BLOCKS, VIRT), jnp.float32) ** steps_of(keys[2], (BLOCKS, VIRT), ((0, 64),), -0.2, 0.2), 0.5, 4.0)
    partners = draw_partners(jax.random.fold_in(keys[4], 71), 0)
    return {"ints": ints, "occ_energy": occ_energy, "vir_energy": vir_energy, "partners": partners}


def reference(ints, occ_energy, vir_energy, partners):
    level = (vir_energy[:, None, :] - occ_energy[:, :, None]).reshape(BLOCKS, PAIR_ROWS)
    start_gamma = jnp.zeros((BLOCKS, PAIR_ROWS, AUX), jnp.float32)

    def visit(gamma, index):
        block_i = lax.dynamic_index_in_dim(ints, index, 0, keepdims=False)
        level_i = lax.dynamic_index_in_dim(level, index, 0, keepdims=False)
        for slot in range(REACH):
            target = partners[index, slot]
            live = target >= 0
            safe = jnp.maximum(target, 0).astype(jnp.int32)
            block_j = lax.dynamic_index_in_dim(ints, safe, 0, keepdims=False)
            level_j = lax.dynamic_index_in_dim(level, safe, 0, keepdims=False)
            pair_ints = jnp.dot(block_i, block_j.T, preferred_element_type=jnp.float32)
            amplitudes = jnp.where(live, pair_ints / (level_i[:, None] + level_j[None, :]), 0.0).astype(jnp.bfloat16)
            gamma = gamma.at[index].add(jnp.dot(amplitudes, block_j, preferred_element_type=jnp.float32))
            gamma = gamma.at[safe].add(jnp.dot(amplitudes.T, block_i, preferred_element_type=jnp.float32))
        return gamma, None

    gamma, unused = lax.scan(visit, start_gamma, jnp.arange(BLOCKS, dtype=jnp.int32))
    return gamma
```

```python
import functools

import jax
import jax.numpy as jnp
from jax import lax
from jax.experimental import pallas as pl
from jax.experimental.pallas import tpu as pltpu
from jax.sharding import PartitionSpec as P

MESH = pl.DeviceIdType.MESH
RING = 4
STEPS = 16
LEFT, RIGHT, FAR, CROSS, WRAP, RELAY, CHUNKS = 0, 8, 16, 24, 32, 36, 40

NT = (((1,), (1,)), ((), ()))


def kernel(
    n, ints_ref, occ_ref, vir_ref, par_ref, out_ref,
    own, nb, gamma, pbuf, xsend, xrecv, abuf, levcol, meta_own, meta_nb,
    send_sem, recv_sem, xs_sem, xr_sem, ms_sem, mr_sem, own_sem, out_sem,
):
    rows, aux = ints_ref.shape
    chunk = rows // 8
    step_rows = rows // 4
    virt = vir_ref.shape[1]
    me = lax.axis_index("occ")
    core = lax.axis_index("aux")
    x = me % RING
    right = me - x + (x + 1) % RING
    left = me - x + (x + RING - 1) % RING
    ymain = (me + n + RING - 2 * RING * (x // 2)) % n
    yback = (me + n - RING + 2 * RING * (x // 2)) % n
    near = ((me + 1) % n, (me + n - 1) % n, (me + 2) % n, (me + n - 2) % n)
    edge = (x == 0) | (x == RING - 1)

    def own_chunk(i):
        return ints_ref.at[pl.ds(pl.multiple_of(i * chunk, chunk), chunk)]

    def nb_chunk(i):
        return nb.at[pl.ds(pl.multiple_of(i * chunk, chunk), chunk)]

    def copy(src, to, ssem, device):
        return pltpu.make_async_remote_copy(
            src_ref=src, dst_ref=nb_chunk(to), send_sem=send_sem.at[ssem], recv_sem=recv_sem.at[to],
            device_id=(device, core), device_id_type=MESH,
        )

    def arrive(i):
        copy(nb_chunk(i), i, 0, right).wait_recv()

    def meta_copy(k, device):
        return pltpu.make_async_remote_copy(
            src_ref=meta_own, dst_ref=meta_nb.at[k], send_sem=ms_sem.at[k], recv_sem=mr_sem.at[k],
            device_id=(device, core), device_id_type=MESH,
        )

    def exchange(s):
        return pltpu.make_async_remote_copy(
            src_ref=xsend.at[s % 2], dst_ref=xrecv.at[s], send_sem=xs_sem.at[s], recv_sem=xr_sem.at[s],
            device_id=(me, 1 - core), device_id_type=MESH,
        )

    load = pltpu.make_async_copy(ints_ref, own, own_sem)
    load.start()

    barrier = pltpu.get_barrier_semaphore()
    for device in (right, left, ymain, yback, *near):
        pl.semaphore_signal(barrier, inc=1, device_id=(device, core), device_id_type=MESH)
    pl.semaphore_signal(barrier, inc=1, device_id=(me, 1 - core), device_id_type=MESH)
    pl.semaphore_wait(barrier, 9)

    @pl.loop(0, 4)
    def _(i):
        copy(own_chunk(i), LEFT + i, i, right).start()
        copy(own_chunk(4 + i), RIGHT + 4 + i, 12 + i, left).start()

        @pl.when(edge)
        def _():
            copy(own_chunk(4 * (x // 2) + i), RELAY + i, 36 + i, yback).start()

    for i in range(rows // virt):
        meta_own[0:1, i * virt : (i + 1) * virt] = vir_ref[...] - occ_ref[0, i]
    for reach in (1, 2):
        listed = (par_ref[0, 0] == me + reach) | (par_ref[0, 1] == me + reach)
        meta_own[reach : reach + 1, :] = jnp.full((1, rows), jnp.where(listed, 1.0, 0.0), jnp.float32)
    meta_own[3:8, :] = jnp.zeros((5, rows), jnp.float32)
    for k, device in enumerate(near):
        meta_copy(k, device).start()
    levcol[...] = jnp.broadcast_to(meta_own[0:1, :], (levcol.shape[1], rows)).T

    @pl.loop(0, 4)
    def _(i):
        here = pl.ds(pl.multiple_of(i * step_rows, step_rows), step_rows)
        gamma[here] = jnp.zeros((step_rows, aux), jnp.float32)

    for k in range(4):
        meta_copy(k, right).wait_recv()
    meta_nb[0, 3:4, :] = meta_nb[0, 1:2, :]
    meta_nb[1, 3:4, :] = meta_own[1:2, :]
    meta_nb[2, 3:4, :] = meta_nb[2, 2:3, :]
    meta_nb[3, 3:4, :] = meta_own[2:3, :]
    load.wait()

    def pass_along_ring(i):
        arrive(LEFT + i)
        copy(nb_chunk(LEFT + i), FAR + i, 4 + i, right).start()
        arrive(RIGHT + 4 + i)
        copy(nb_chunk(RIGHT + 4 + i), FAR + 4 + i, 16 + i, left).start()

        @pl.when(edge)
        def _():
            copy(nb_chunk(4 * x + i), WRAP + i, 32 + i, ymain).start()

    def rest_of_own(i):
        @pl.when(x < RING - 1)
        def _():
            copy(own_chunk(4 + i), LEFT + 4 + i, 8 + i, right).start()

        @pl.when(x > 0)
        def _():
            copy(own_chunk(i), RIGHT + i, 20 + i, left).start()

        @pl.when(edge)
        def _():
            arrive(RELAY + i)

        @pl.when(x == RING - 1)
        def _():
            copy(nb_chunk(RELAY + i), LEFT + 4 + i, 8 + i, right).start()

        @pl.when(x == 0)
        def _():
            copy(nb_chunk(RELAY + i), RIGHT + i, 20 + i, left).start()

    def pass_across(i):
        arrive(FAR + i)
        copy(nb_chunk(FAR + i), CROSS + i, 24 + i, ymain).start()
        arrive(FAR + 4 + i)
        copy(nb_chunk(FAR + 4 + i), CROSS + 4 + i, 28 + i, ymain).start()

    first = 1 - (x + 3) // 4
    last = (x + 1) // 4

    def place(s):
        early = 1 - s // 8
        quad0 = 1 - (s // 4 + 3) // 4
        quad1 = early - quad0
        h = s % 2
        late = s // 8
        kind = s % 4
        pair = kind // 2
        part = 2 * (early * ((s // 2) % 2) + late * ((s // 4) % 2))
        swap = (1 - h) * first + h * last
        at0 = (1 - swap) * (h * (RIGHT + 4)) + swap * WRAP
        in0 = 4 * h
        at1 = FAR + 4 * h
        at2 = (1 - pair) * (CROSS + 4 * h) + pair * ((1 - h) * (LEFT + 4) + h * RIGHT)
        in2 = (1 - pair) * (4 * h) + pair * (4 * (1 - h))
        at = quad0 * at0 + quad1 * at1 + late * at2 + part
        inside = quad0 * in0 + quad1 * (4 * h) + late * in2 + part
        slot = quad0 * h + quad1 * (3 - x // 2) + late * ((1 - pair) * (2 + x // 2) + pair * h)
        waits = quad0 * swap + late
        return at, inside, slot, waits

    def block_rows(at):
        return pl.ds(pl.multiple_of(at * chunk, chunk), step_rows)

    m_rows = rows // 2
    n_cols = aux // 4

    def products(s):
        at, inside, slot, waits = place(s)

        @pl.when(waits == 1)
        def _():
            arrive(at)
            arrive(at + 1)

        @pl.when(s >= 2)
        def _():
            exchange(s - 2).wait_send()

        @pl.loop(0, rows // m_rows)
        def _(m):
            here = pl.ds(pl.multiple_of(m * m_rows, m_rows), m_rows)
            part = lax.dot_general(own[here], nb[block_rows(at)], NT, preferred_element_type=jnp.float32)
            pbuf[s % 2, here] = part
            xsend[s % 2, here] = part.astype(jnp.bfloat16)

        exchange(s).start()

    def finish(s):
        at, inside, slot, waits = place(s)
        exchange(s).wait_recv()
        cols = pl.ds(pl.multiple_of(inside * chunk, chunk), step_rows)
        level = meta_nb[slot, 0:1, cols]
        live = meta_nb[slot, 3:4, cols]
        wide = step_rows // levcol.shape[1]

        @pl.loop(0, 4)
        def _(m):
            here = pl.ds(pl.multiple_of(m * step_rows, step_rows), step_rows)
            total = pbuf[s % 2, here] + xrecv[s, here].astype(jnp.float32)
            mine = levcol[here]
            mine = jnp.concatenate([mine] * wide, axis=1)
            abuf[here] = jnp.where(live > 0.5, total / (mine + level), 0.0).astype(jnp.bfloat16)

        @pl.loop(0, aux // n_cols)
        def _(c):
            there = pl.ds(pl.multiple_of(c * n_cols, n_cols), n_cols)
            gamma[:, there] += jnp.dot(abuf[...], nb[block_rows(at), there], preferred_element_type=jnp.float32)

    @pl.loop(0, STEPS + 1)
    def _(s):
        @pl.when(s == 0)
        def _():
            pl.loop(0, 3)(pass_along_ring)

        @pl.when(s == 2)
        def _():
            pl.loop(3, 4)(pass_along_ring)
            pl.loop(0, 4)(rest_of_own)

        @pl.when(s == 4)
        def _():
            pl.loop(0, 2)(pass_across)

        @pl.when(s == 6)
        def _():
            pl.loop(2, 4)(pass_across)

        @pl.when(s < STEPS)
        def _():
            products(s)

        @pl.when(s >= 1)
        def _():
            finish(s - 1)

    store = pltpu.make_async_copy(gamma, out_ref, out_sem)
    store.start()

    @pl.loop(0, 32)
    def _(k):
        copy(nb_chunk(0), 0, k, right).wait_send()

    @pl.when(edge)
    def _():
        @pl.loop(32, 40)
        def _(k):
            copy(nb_chunk(0), 0, k, right).wait_send()

    for k in range(4):
        meta_copy(k, right).wait_send()
    exchange(STEPS - 2).wait_send()
    exchange(STEPS - 1).wait_send()
    store.wait()


def body(n, ints, occ_energy, vir_energy, partners):
    _, rows, aux = ints.shape
    lanes = min(128, rows // 4)
    step_rows = rows // 4
    result = pl.pallas_call(
        functools.partial(kernel, n),
        out_shape=jax.ShapeDtypeStruct((rows, aux), jnp.float32),
        in_specs=[
            pl.BlockSpec(memory_space=pl.ANY),
            pl.BlockSpec(memory_space=pltpu.SMEM),
            pl.BlockSpec(memory_space=pltpu.VMEM),
            pl.BlockSpec(memory_space=pltpu.SMEM),
        ],
        out_specs=pl.BlockSpec(memory_space=pl.ANY),
        scratch_shapes=[
            pltpu.VMEM((rows, aux), jnp.bfloat16),
            pltpu.VMEM((CHUNKS * rows // 8, aux), jnp.bfloat16),
            pltpu.VMEM((rows, aux), jnp.float32),
            pltpu.VMEM((2, rows, step_rows), jnp.float32),
            pltpu.VMEM((2, rows, step_rows), jnp.bfloat16),
            pltpu.VMEM((STEPS, rows, step_rows), jnp.bfloat16),
            pltpu.VMEM((rows, step_rows), jnp.bfloat16),
            pltpu.VMEM((rows, lanes), jnp.float32),
            pltpu.VMEM((8, rows), jnp.float32),
            pltpu.VMEM((4, 8, rows), jnp.float32),
            pltpu.SemaphoreType.DMA((40,)),
            pltpu.SemaphoreType.DMA((CHUNKS,)),
            pltpu.SemaphoreType.DMA((STEPS,)),
            pltpu.SemaphoreType.DMA((STEPS,)),
            pltpu.SemaphoreType.DMA((4,)),
            pltpu.SemaphoreType.DMA((4,)),
            pltpu.SemaphoreType.DMA,
            pltpu.SemaphoreType.DMA,
        ],
        compiler_params=pltpu.CompilerParams(
            collective_id=0, has_side_effects=True, vmem_limit_bytes=56 * 2**20
        ),
        cost_estimate=pl.CostEstimate(
            flops=16 * rows * rows * aux, bytes_accessed=6 * rows * aux, transcendentals=0
        ),
    )(ints[0], occ_energy, vir_energy, partners)
    return result[None]


def solution(mesh):
    return jax.shard_map(
        functools.partial(body, mesh.shape["occ"]),
        mesh=mesh,
        in_specs=(P("occ", None, "aux"), P("occ", None), P("occ", None), P("occ", None)),
        out_specs=P("occ", None, "aux"),
        check_vma=False,
    )
```

```python
import functools

import jax
import jax.numpy as jnp
from jax import lax
from jax.experimental import pallas as pl
from jax.experimental.pallas import tpu as pltpu
from jax.sharding import PartitionSpec as P

MESH = pl.DeviceIdType.MESH
RING = 4
PARTS = 16
HALF = PARTS // 2
TICKS = 3 * HALF
AHEAD = 2
STEPS = 18
LEFT, RIGHT, FAR, CROSS, WRAP, RELAY, CHUNKS = 0, 16, 32, 48, 64, 72, 80
TO_RIGHT, TO_LEFT, TO_CROSS, TO_WRAP, TO_RELAY, SENDS = 0, 24, 48, 64, 72, 80

NT = (((1,), (1,)), ((), ()))


def kernel(
    n, ints_ref, occ_ref, vir_ref, par_ref, gamma,
    own, nb, pbuf, xsend, xrecv, abuf, levcol, meta_own, meta_nb,
    send_sem, recv_sem, xs_sem, xr_sem, ms_sem, mr_sem, own_sem,
):
    rows, aux = ints_ref.shape
    chunk = rows // PARTS
    step_rows = rows // 4
    virt = vir_ref.shape[1]
    me = lax.axis_index("occ")
    core = lax.axis_index("aux")
    x = me % RING
    right = me - x + (x + 1) % RING
    left = me - x + (x + RING - 1) % RING
    ymain = (me + n + RING - 2 * RING * (x // 2)) % n
    yback = (me + n - RING + 2 * RING * (x // 2)) % n
    near = ((me + 1) % n, (me + n - 1) % n, (me + 2) % n, (me + n - 2) % n)
    edge = (x == 0) | (x == RING - 1)

    def own_chunk(i):
        return ints_ref.at[pl.ds(pl.multiple_of(i * chunk, chunk), chunk)]

    def nb_chunk(i):
        return nb.at[pl.ds(pl.multiple_of(i * chunk, chunk), chunk)]

    def copy(src, to, ssem, device):
        return pltpu.make_async_remote_copy(
            src_ref=src, dst_ref=nb_chunk(to), send_sem=send_sem.at[ssem], recv_sem=recv_sem.at[to],
            device_id=(device, core), device_id_type=MESH,
        )

    def arrive(i):
        copy(nb_chunk(i), i, 0, right).wait_recv()

    def meta_copy(k, device):
        return pltpu.make_async_remote_copy(
            src_ref=meta_own, dst_ref=meta_nb.at[k], send_sem=ms_sem.at[k], recv_sem=mr_sem.at[k],
            device_id=(device, core), device_id_type=MESH,
        )

    def exchange(t):
        step = 3 * (t // 4 - 1) + t % 4
        return pltpu.make_async_remote_copy(
            src_ref=xsend.at[t % 4], dst_ref=xrecv.at[step], send_sem=xs_sem.at[step], recv_sem=xr_sem.at[step],
            device_id=(me, 1 - core), device_id_type=MESH,
        )

    load = pltpu.make_async_copy(ints_ref, own, own_sem)
    load.start()

    barrier = pltpu.get_barrier_semaphore()
    for device in (right, left, ymain, yback, *near):
        pl.semaphore_signal(barrier, inc=1, device_id=(device, core), device_id_type=MESH)
    pl.semaphore_signal(barrier, inc=1, device_id=(me, 1 - core), device_id_type=MESH)
    pl.semaphore_wait(barrier, 9)

    def send_on_ring(k):
        @pl.when(k < HALF)
        def _():
            copy(own_chunk(k), LEFT + k, TO_RIGHT + k, right).start()
            copy(own_chunk(HALF + k), RIGHT + HALF + k, TO_LEFT + k, left).start()

        @pl.when((k >= HALF) & (k < 2 * HALF))
        def _():
            i = k - HALF
            copy(nb_chunk(LEFT + i), FAR + i, TO_RIGHT + k, right).start()
            copy(nb_chunk(RIGHT + HALF + i), FAR + HALF + i, TO_LEFT + k, left).start()

        @pl.when((k >= 2 * HALF) & (k < TICKS))
        def _():
            i = k - 2 * HALF

            @pl.when(x < RING - 1)
            def _():
                copy(own_chunk(HALF + i), LEFT + HALF + i, TO_RIGHT + k, right).start()

            @pl.when(x > 0)
            def _():
                copy(own_chunk(i), RIGHT + i, TO_LEFT + k, left).start()

            @pl.when(edge)
            def _():
                arrive(RELAY + i)

            @pl.when(x == RING - 1)
            def _():
                copy(nb_chunk(RELAY + i), LEFT + HALF + i, TO_RIGHT + k, right).start()

            @pl.when(x == 0)
            def _():
                copy(nb_chunk(RELAY + i), RIGHT + i, TO_LEFT + k, left).start()

    pl.loop(0, AHEAD)(send_on_ring)

    @pl.when(edge)
    def _():
        @pl.loop(0, HALF)
        def _(i):
            copy(own_chunk(HALF * (x // 2) + i), RELAY + i, TO_RELAY + i, yback).start()

    for i in range(rows // virt):
        meta_own[0:1, i * virt : (i + 1) * virt] = vir_ref[...] - occ_ref[0, i]
    for reach in (1, 2):
        listed = (par_ref[0, 0] == me + reach) | (par_ref[0, 1] == me + reach)
        meta_own[reach : reach + 1, :] = jnp.full((1, rows), jnp.where(listed, 1.0, 0.0), jnp.float32)
    meta_own[3:8, :] = jnp.zeros((5, rows), jnp.float32)
    for k, device in enumerate(near):
        meta_copy(k, device).start()
    levcol[...] = jnp.broadcast_to(meta_own[0:1, :], (levcol.shape[1], rows)).T

    @pl.loop(0, 4)
    def _(i):
        here = pl.ds(pl.multiple_of(i * step_rows, step_rows), step_rows)
        gamma[here] = jnp.zeros((step_rows, aux), jnp.float32)

    for k in range(4):
        meta_copy(k, right).wait_recv()
    meta_nb[0, 3:4, :] = meta_nb[0, 1:2, :]
    meta_nb[1, 3:4, :] = meta_own[1:2, :]
    meta_nb[2, 3:4, :] = meta_nb[2, 2:3, :]
    meta_nb[3, 3:4, :] = meta_own[2:3, :]
    load.wait()

    def send_across(j):
        i = HALF * ((j // 4) % 2) + 4 * (j // 8) + j % 4
        copy(nb_chunk(FAR + i), CROSS + i, TO_CROSS + j, ymain).start()

    def links(t):
        @pl.when(t < 2 * HALF)
        def _():
            arrive(LEFT + t + (t // HALF) * (FAR - LEFT - HALF))
            arrive(RIGHT + HALF + t + (t // HALF) * (FAR - RIGHT - HALF))

        @pl.when(edge & (t < HALF))
        def _():
            copy(nb_chunk((RIGHT + HALF) // 3 * x + t), WRAP + t, TO_WRAP + t, ymain).start()

        @pl.when((t >= HALF) & (t < HALF + 4))
        def _():
            send_across(t - HALF)

        @pl.when((t >= HALF + 3) & (t < 3 * HALF - 1))
        def _():
            send_across(t - HALF + 1)

        copy(nb_chunk(0), 0, TO_RIGHT + t, right).wait_send()
        copy(nb_chunk(0), 0, TO_LEFT + t, left).wait_send()
        send_on_ring(t + AHEAD)

    first = 1 - (x + 3) // 4
    last = (x + 1) // 4

    def has_step(t):
        return (t >= 5) & (t < 27) & (t % 4 < 3) & ((t >= 12) | (t % 4 > 0))

    def place(t):
        q, r = t // 4, t % 4
        q12 = (8 - q) // 6
        q56 = (q + 1) // 6
        q34 = 1 - q12 - q56
        r2 = r // 2
        r1 = r % 2
        r0 = 1 - r1 - r2
        swap = r1 * first + r2 * last
        across = (1 - q12) * r2
        g = q - 3
        at = (
            q12 * (r2 * (1 - swap) * (RIGHT + HALF) + swap * WRAP + 4 * (q - 1))
            + across * (CROSS + HALF * (g % 2) + 4 * (g // 2))
            + q34 * (1 - r2) * (FAR + HALF * r1 + 4 * (q - 3))
            + q56 * (1 - r2) * (r0 * (LEFT + HALF) + r1 * RIGHT + 4 * (q - 5))
        )
        inside = (
            q12 * (r2 * HALF + 4 * (q - 1))
            + across * (HALF * (g % 2) + 4 * (g // 2))
            + q34 * (1 - r2) * (HALF * r1 + 4 * (q - 3))
            + q56 * (1 - r2) * (r0 * HALF + 4 * (q - 5))
        )
        slot = q12 * r2 + across * (2 + x // 2) + q34 * (1 - r2) * (3 - x // 2) + q56 * (1 - r2) * r1
        waits = q12 * swap + across + q56 * (1 - r2)
        return at, inside, slot, waits

    def block_rows(at):
        return pl.ds(pl.multiple_of(at * chunk, chunk), step_rows)

    m_rows = rows // 2
    n_cols = aux // 4

    def products(t):
        at, inside, slot, waits = place(t)

        @pl.when(waits == 1)
        def _():
            pl.loop(0, 4)(lambda i: arrive(at + i))

        @pl.when(has_step(t - 4))
        def _():
            exchange(t - 4).wait_send()

        @pl.loop(0, rows // m_rows)
        def _(m):
            here = pl.ds(pl.multiple_of(m * m_rows, m_rows), m_rows)
            part = lax.dot_general(own[here], nb[block_rows(at)], NT, preferred_element_type=jnp.float32)
            pbuf[t % 4, here] = part
            xsend[t % 4, here] = part.astype(jnp.bfloat16)

        exchange(t).start()

    def finish(t):
        at, inside, slot, waits = place(t)
        exchange(t).wait_recv()
        cols = pl.ds(pl.multiple_of(inside * chunk, step_rows), step_rows)
        level = meta_nb[slot, 0:1, cols]
        live = meta_nb[slot, 3:4, cols]
        wide = step_rows // levcol.shape[1]
        step = 3 * (t // 4 - 1) + t % 4

        @pl.loop(0, 4)
        def _(m):
            here = pl.ds(pl.multiple_of(m * step_rows, step_rows), step_rows)
            total = pbuf[t % 4, here] + xrecv[step, here].astype(jnp.float32)
            mine = levcol[here]
            mine = jnp.concatenate([mine] * wide, axis=1)
            abuf[here] = jnp.where(live > 0.5, total / (mine + level), 0.0).astype(jnp.bfloat16)

        @pl.loop(0, aux // n_cols)
        def _(c):
            there = pl.ds(pl.multiple_of(c * n_cols, n_cols), n_cols)
            gamma[:, there] += jnp.dot(abuf[...], nb[block_rows(at), there], preferred_element_type=jnp.float32)

    @pl.loop(0, 28)
    def _(t):
        @pl.when(t < TICKS)
        def _():
            links(t)

        @pl.when(has_step(t))
        def _():
            products(t)

        @pl.when(has_step(t - 1))
        def _():
            finish(t - 1)

    @pl.loop(TO_CROSS, TO_WRAP)
    def _(k):
        copy(nb_chunk(0), 0, k, right).wait_send()

    @pl.when(edge)
    def _():
        @pl.loop(TO_WRAP, SENDS)
        def _(k):
            copy(nb_chunk(0), 0, k, right).wait_send()

    for k in range(4):
        meta_copy(k, right).wait_send()
    for t in (24, 25, 26):
        exchange(t).wait_send()


def body(n, ints, occ_energy, vir_energy, partners):
    _, rows, aux = ints.shape
    lanes = min(128, rows // 4)
    step_rows = rows // 4
    result = pl.pallas_call(
        functools.partial(kernel, n),
        out_shape=pltpu.VMEM((rows, aux), jnp.float32),
        in_specs=[
            pl.BlockSpec(memory_space=pl.ANY),
            pl.BlockSpec(memory_space=pltpu.SMEM),
            pl.BlockSpec(memory_space=pltpu.VMEM),
            pl.BlockSpec(memory_space=pltpu.SMEM),
        ],
        out_specs=pl.BlockSpec(memory_space=pltpu.VMEM),
        scratch_shapes=[
            pltpu.VMEM((rows, aux), jnp.bfloat16),
            pltpu.VMEM((CHUNKS * rows // PARTS, aux), jnp.bfloat16),
            pltpu.VMEM((3, rows, step_rows), jnp.float32),
            pltpu.VMEM((3, rows, step_rows), jnp.bfloat16),
            pltpu.VMEM((STEPS, rows, step_rows), jnp.bfloat16),
            pltpu.VMEM((rows, step_rows), jnp.bfloat16),
            pltpu.VMEM((rows, lanes), jnp.float32),
            pltpu.VMEM((8, rows), jnp.float32),
            pltpu.VMEM((4, 8, rows), jnp.float32),
            pltpu.SemaphoreType.DMA((SENDS,)),
            pltpu.SemaphoreType.DMA((CHUNKS,)),
            pltpu.SemaphoreType.DMA((STEPS,)),
            pltpu.SemaphoreType.DMA((STEPS,)),
            pltpu.SemaphoreType.DMA((4,)),
            pltpu.SemaphoreType.DMA((4,)),
            pltpu.SemaphoreType.DMA,
        ],
        compiler_params=pltpu.CompilerParams(
            collective_id=0, has_side_effects=True, vmem_limit_bytes=44 * 2**20
        ),
        cost_estimate=pl.CostEstimate(
            flops=16 * rows * rows * aux, bytes_accessed=6 * rows * aux, transcendentals=0
        ),
    )(ints[0], occ_energy, vir_energy, partners)
    return result[None]


def solution(mesh):
    return jax.shard_map(
        functools.partial(body, mesh.shape["occ"]),
        mesh=mesh,
        in_specs=(P("occ", None, "aux"), P("occ", None), P("occ", None), P("occ", None)),
        out_specs=P("occ", None, "aux"),
        check_vma=False,
    )
```

```python
import functools

import jax
import jax.numpy as jnp
from jax import lax
from jax.experimental import pallas as pl
from jax.experimental.pallas import tpu as pltpu
from jax.sharding import PartitionSpec as P

MESH = pl.DeviceIdType.MESH
RING = 4
PARTS = 32
HALF = PARTS // 2
STEP = PARTS // 4
TICKS = 3 * HALF
AHEAD = 3
STEPS = 16
LEFT, RIGHT, FAR, CROSS, WRAP, RELAY, CHUNKS = (i * HALF for i in (0, 2, 4, 6, 8, 9, 10))
TURN = 8
TO_RIGHT, TO_LEFT, TO_CROSS, TO_WRAP = 0, TURN, 2 * TURN, 2 * TURN + 2 * HALF
TO_RELAY, SENDS = TO_WRAP + HALF, TO_WRAP + 2 * HALF

NT = (((1,), (1,)), ((), ()))


def kernel(
    n, ints_ref, occ_in, vir_in, par_in, gamma,
    occ_ref, vir_ref, par_ref, own, nb, pbuf, xsend, xrecv, abuf, levcol, meta_own, meta_nb,
    send_sem, recv_sem, xs_sem, xr_sem, ms_sem, mr_sem, own_sem, in_sem,
):
    rows, aux = ints_ref.shape
    chunk = rows // PARTS
    step_rows = rows // 4
    virt = vir_ref.shape[1]
    me = lax.axis_index("occ")
    core = lax.axis_index("aux")
    x = me % RING
    right = me - x + (x + 1) % RING
    left = me - x + (x + RING - 1) % RING
    ymain = (me + n + RING - 2 * RING * (x // 2)) % n
    yback = (me + n - RING + 2 * RING * (x // 2)) % n
    near = ((me + 1) % n, (me + n - 1) % n, (me + 2) % n, (me + n - 2) % n)
    edge = (x == 0) | (x == RING - 1)

    first = 1 - (x + 3) // 4
    last = (x + 1) // 4

    def after(k):
        return (me + n - k) // n

    def before(k):
        return (2 * n - 1 - k - me) // n

    has_main = (1 - x // 2) * before(RING) + (x // 2) * after(RING)
    has_back = (1 - x // 2) * after(RING) + (x // 2) * before(RING)
    has_near = (before(1), after(1), before(2), after(2))
    edge_main = edge & (has_main == 1)
    edge_back = edge & (has_back == 1)

    def own_chunk(i):
        return ints_ref.at[pl.ds(pl.multiple_of(i * chunk, chunk), chunk)]

    def nb_chunk(i):
        return nb.at[pl.ds(pl.multiple_of(i * chunk, chunk), chunk)]

    def copy(src, to, ssem, device):
        return pltpu.make_async_remote_copy(
            src_ref=src, dst_ref=nb_chunk(to), send_sem=send_sem.at[ssem], recv_sem=recv_sem.at[to],
            device_id=(device, core), device_id_type=MESH,
        )

    def arrive(i):
        copy(nb_chunk(i), i, 0, right).wait_recv()

    def meta_copy(k, device):
        return pltpu.make_async_remote_copy(
            src_ref=meta_own, dst_ref=meta_nb.at[k], send_sem=ms_sem.at[k], recv_sem=mr_sem.at[k],
            device_id=(device, core), device_id_type=MESH,
        )

    def exchange(s):
        return pltpu.make_async_remote_copy(
            src_ref=xsend.at[s % 2], dst_ref=xrecv.at[s], send_sem=xs_sem.at[s], recv_sem=xr_sem.at[s],
            device_id=(me, 1 - core), device_id_type=MESH,
        )

    load = pltpu.make_async_copy(ints_ref, own, own_sem)
    load.start()
    small = [
        pltpu.make_async_copy(src, dst, in_sem.at[i])
        for i, (src, dst) in enumerate(((occ_in, occ_ref), (vir_in, vir_ref), (par_in, par_ref)))
    ]
    for item in small:
        item.start()

    barrier = pltpu.get_barrier_semaphore()
    def greet(device, other):
        pl.semaphore_signal(barrier, inc=1, device_id=(device, other), device_id_type=MESH)

    greet(right, core)
    greet(left, core)
    greet(me, 1 - core)
    for device, there in zip((ymain, yback, *near), (has_main, has_back, *has_near)):
        pl.when(there == 1)(functools.partial(greet, device, core))
    pl.semaphore_wait(barrier, 3 + has_main + has_back + sum(has_near))

    alternate = 2 * HALF - 3

    def on_own(k, act):
        @pl.when(k < 3)
        def _():
            act(k)

        @pl.when((k >= 3) & (k < alternate) & (k % 2 == 0))
        def _():
            act((k + 2) // 2)

    def on_passed(k, act, end=2 * HALF):
        @pl.when((k >= 3) & (k < alternate) & (k % 2 == 1))
        def _():
            act((k - 3) // 2)

        @pl.when((k >= alternate) & (k < end))
        def _():
            act(k - HALF)

    def send_on_ring(k):
        turn = k % TURN

        def own_first(i):
            copy(own_chunk(i), LEFT + i, TO_RIGHT + turn, right).start()
            copy(own_chunk(HALF + i), RIGHT + HALF + i, TO_LEFT + turn, left).start()

        def passed(i):
            copy(nb_chunk(LEFT + i), FAR + i, TO_RIGHT + turn, right).start()
            copy(nb_chunk(RIGHT + HALF + i), FAR + HALF + i, TO_LEFT + turn, left).start()

        on_own(k, own_first)
        on_passed(k, passed)

        @pl.when((k >= 2 * HALF) & (k < TICKS))
        def _():
            i = k - 2 * HALF

            @pl.when(x < RING - 1)
            def _():
                copy(own_chunk(HALF + i), LEFT + HALF + i, TO_RIGHT + turn, right).start()

            @pl.when(x > 0)
            def _():
                copy(own_chunk(i), RIGHT + i, TO_LEFT + turn, left).start()

            @pl.when(edge_main)
            def _():
                arrive(RELAY + i)

            @pl.when((x == RING - 1) & (has_main == 1))
            def _():
                copy(nb_chunk(RELAY + i), LEFT + HALF + i, TO_RIGHT + turn, right).start()

            @pl.when((x == 0) & (has_main == 1))
            def _():
                copy(nb_chunk(RELAY + i), RIGHT + i, TO_LEFT + turn, left).start()

    pl.loop(0, AHEAD)(send_on_ring)

    @pl.when(edge_back)
    def _():
        @pl.loop(0, HALF)
        def _(i):
            copy(own_chunk(HALF * (x // 2) + i), RELAY + i, TO_RELAY + i, yback).start()

    for item in small:
        item.wait()
    for i in range(rows // virt):
        meta_own[0:1, i * virt : (i + 1) * virt] = vir_ref[...] - occ_ref[0:1, i : i + 1]
    for reach in (1, 2):
        found = [jnp.where(par_ref[0:1, i : i + 1] == me + reach, 1.0, 0.0) for i in range(2)]
        meta_own[reach : reach + 1, :] = jnp.broadcast_to(jnp.maximum(*found), (1, rows))
    meta_own[3:8, :] = jnp.zeros((5, rows), jnp.float32)
    for k, device in enumerate(near):
        pl.when(has_near[k] == 1)(meta_copy(k, device).start)
    levcol[...] = jnp.broadcast_to(meta_own[0:1, :], (levcol.shape[1], rows)).T

    @pl.loop(0, 4)
    def _(i):
        here = pl.ds(pl.multiple_of(i * step_rows, step_rows), step_rows)
        gamma[here] = jnp.zeros((step_rows, aux), jnp.float32)

    has_slot = (after(1), before(1), after(2), before(2))
    for k in range(4):

        @pl.when(has_slot[k] == 1)
        def _():
            meta_copy(k, right).wait_recv()
            listed = 1 + k // 2
            meta_nb[k, 3:4, :] = meta_own[listed : listed + 1, :] if k % 2 else meta_nb[k, listed : listed + 1, :]

    load.wait()

    def send_across(j):
        group = j // STEP
        i = HALF * (group % 2) + STEP * (group // 2) + j % STEP

        @pl.when(has_main == 1)
        def _():
            copy(nb_chunk(FAR + i), CROSS + i, TO_CROSS + j, ymain).start()

    def links(t):
        def own_first(i):
            arrive(LEFT + i)
            arrive(RIGHT + HALF + i)

            @pl.when(edge_main)
            def _():
                copy(nb_chunk((RIGHT + HALF) // 3 * x + i), WRAP + i, TO_WRAP + i, ymain).start()

        def passed(i):
            arrive(FAR + i)
            arrive(FAR + HALF + i)

        relayed = t // (2 * HALF)

        @pl.when((1 - has_main) * relayed * last == 0)
        def _():
            copy(nb_chunk(0), 0, TO_RIGHT + t % TURN, right).wait_send()

        @pl.when((1 - has_main) * relayed * first == 0)
        def _():
            copy(nb_chunk(0), 0, TO_LEFT + t % TURN, left).wait_send()

        on_own(t, own_first)
        on_passed(t, passed)
        send_on_ring(t + AHEAD)
        on_passed(t, send_across, TICKS)


    def ticks_before(s):
        return 7 + s + (s + 14) // 16 + 2 * ((s + 11) // 16)

    def place(s):
        late = (s + 6) // 16
        early = 1 - late
        p = early * (s // 5) + late * ((s - 10) // 3)
        r = early * (s % 5) + late * (2 * ((s - 10) % 3))
        across = r // 4
        r2 = (r // 2) * (1 - across)
        h = r % 2
        base = (1 - across) * (1 - r2)
        swap = early * base * ((1 - h) * first + h * last)
        group = p + 2 * late
        at = (
            early * base * (1 - swap) * h * (RIGHT + HALF)
            + swap * WRAP
            + early * r2 * (FAR + HALF * h)
            + late * base * (LEFT + HALF)
            + late * r2 * RIGHT
            + (1 - across) * STEP * p
            + across * (CROSS + HALF * (group % 2) + STEP * (group // 2))
        )
        inside = (
            (1 - across) * (HALF * (early * h + late * base) + STEP * p)
            + across * (HALF * (group % 2) + STEP * (group // 2))
        )
        slot = early * (base * h + r2 * (3 - x // 2)) + late * r2 + across * (2 + x // 2)
        waits = swap + across + late * (1 - across)
        foreign = swap + across + late * (base * first + r2 * last)
        return at, inside, slot, waits, 1 - foreign * (1 - has_back)

    def block_rows(at):
        return pl.ds(pl.multiple_of(at * chunk, chunk), step_rows)

    m_rows = rows // 2
    n_cols = aux // 4

    def sent(s):
        @pl.when(place(s)[4] == 1)
        def _():
            exchange(s).wait_send()

    def products(s):
        at, _, _, waits, _ = place(s)

        @pl.when(waits == 1)
        def _():
            pl.loop(0, STEP)(lambda i: arrive(at + i))

        @pl.loop(0, rows // m_rows)
        def _(m):
            here = pl.ds(pl.multiple_of(m * m_rows, m_rows), m_rows)
            part = lax.dot_general(own[here], nb[block_rows(at)], NT, preferred_element_type=jnp.float32)
            pbuf[s % 2, here] = part
            xsend[s % 2, here] = part.astype(jnp.bfloat16)

        exchange(s).start()

    def finish(s):
        at, inside, slot, _, _ = place(s)
        exchange(s).wait_recv()
        cols = pl.ds(pl.multiple_of(inside * chunk, step_rows), step_rows)
        level = meta_nb[slot, 0:1, cols]
        live = meta_nb[slot, 3:4, cols]
        wide = step_rows // levcol.shape[1]

        @pl.loop(0, 4)
        def _(m):
            here = pl.ds(pl.multiple_of(m * step_rows, step_rows), step_rows)
            total = pbuf[s % 2, here] + xrecv[s, here].astype(jnp.float32)
            mine = levcol[here]
            mine = jnp.concatenate([mine] * wide, axis=1)
            abuf[here] = jnp.where(live > 0.5, total / (mine + level), 0.0).astype(jnp.bfloat16)

        @pl.loop(0, aux // n_cols)
        def _(c):
            there = pl.ds(pl.multiple_of(c * n_cols, n_cols), n_cols)
            gamma[:, there] += jnp.dot(abuf[...], nb[block_rows(at), there], preferred_element_type=jnp.float32)

    fine = PARTS // 16

    def links_until(start, end):
        @pl.loop(start, end)
        def _(t):
            @pl.when(t < TICKS)
            def _():
                links(t)

    links_until(0, fine * ticks_before(0))

    @pl.loop(0, STEPS + 2)
    def _(s):
        now = fine * ticks_before(s)
        made = s - (s + 2) // 16
        ended = s - 1 - (s + 1) // 16

        @pl.when((s != 13) & (made >= 2) & (made < STEPS))
        def _():
            sent(made - 2)

        @pl.when((s != 13) & (made < STEPS))
        def _():
            pl.when(place(made)[4] == 1)(functools.partial(products, made))

        links_until(now, now + 1)

        @pl.when((s != 14) & (ended >= 0))
        def _():
            pl.when(place(ended)[4] == 1)(functools.partial(finish, ended))

        links_until(now + 1, fine * ticks_before(s + 1))

    def sent_all(start, end):
        @pl.loop(start, end)
        def _(k):
            copy(nb_chunk(0), 0, k, right).wait_send()

    pl.when(has_main == 1)(functools.partial(sent_all, TO_CROSS, TO_WRAP))
    pl.when(edge_main)(functools.partial(sent_all, TO_WRAP, TO_RELAY))
    pl.when(edge_back)(functools.partial(sent_all, TO_RELAY, SENDS))
    for k in range(4):
        pl.when(has_near[k] == 1)(meta_copy(k, right).wait_send)
    sent(STEPS - 2)
    sent(STEPS - 1)


def body(n, ints, occ_energy, vir_energy, partners):
    _, rows, aux = ints.shape
    lanes = min(128, rows // 4)
    step_rows = rows // 4
    result = pl.pallas_call(
        functools.partial(kernel, n),
        out_shape=pltpu.VMEM((rows, aux), jnp.float32),
        in_specs=[
            pl.BlockSpec(memory_space=pl.ANY),
            pl.BlockSpec(memory_space=pl.ANY),
            pl.BlockSpec(memory_space=pl.ANY),
            pl.BlockSpec(memory_space=pl.ANY),
        ],
        out_specs=pl.BlockSpec(memory_space=pltpu.VMEM),
        scratch_shapes=[
            pltpu.VMEM(occ_energy.shape, jnp.float32),
            pltpu.VMEM(vir_energy.shape, jnp.float32),
            pltpu.VMEM(partners.shape, jnp.int32),
            pltpu.VMEM((rows, aux), jnp.bfloat16),
            pltpu.VMEM((CHUNKS * rows // PARTS, aux), jnp.bfloat16),
            pltpu.VMEM((2, rows, step_rows), jnp.float32),
            pltpu.VMEM((2, rows, step_rows), jnp.bfloat16),
            pltpu.VMEM((STEPS, rows, step_rows), jnp.bfloat16),
            pltpu.VMEM((rows, step_rows), jnp.bfloat16),
            pltpu.VMEM((rows, lanes), jnp.float32),
            pltpu.VMEM((8, rows), jnp.float32),
            pltpu.VMEM((4, 8, rows), jnp.float32),
            pltpu.SemaphoreType.DMA((SENDS,)),
            pltpu.SemaphoreType.DMA((CHUNKS,)),
            pltpu.SemaphoreType.DMA((STEPS,)),
            pltpu.SemaphoreType.DMA((STEPS,)),
            pltpu.SemaphoreType.DMA((4,)),
            pltpu.SemaphoreType.DMA((4,)),
            pltpu.SemaphoreType.DMA,
            pltpu.SemaphoreType.DMA((3,)),
        ],
        compiler_params=pltpu.CompilerParams(
            collective_id=0, has_side_effects=True, vmem_limit_bytes=55 * 2**20
        ),
        cost_estimate=pl.CostEstimate(
            flops=16 * rows * rows * aux, bytes_accessed=6 * rows * aux, transcendentals=0
        ),
    )(ints[0], occ_energy, vir_energy, partners)
    return result[None]


def solution(mesh):
    return jax.shard_map(
        functools.partial(body, mesh.shape["occ"]),
        mesh=mesh,
        in_specs=(P("occ", None, "aux"), P("occ", None), P("occ", None), P("occ", None)),
        out_specs=P("occ", None, "aux"),
        check_vma=False,
    )
```

```python
import functools

import jax
import jax.numpy as jnp
from jax import lax
from jax.experimental import pallas as pl
from jax.experimental.pallas import tpu as pltpu
from jax.sharding import PartitionSpec as P

MESH = pl.DeviceIdType.MESH
RING = 4
PARTS = 32
HALF = PARTS // 2
STEP = PARTS // 4
TICKS = 3 * HALF
AHEAD = 3
EARLY = 8
LATE = 0
STEPS = 16
LEFT, RIGHT, FAR, CROSS, WRAP, RELAY, CHUNKS = (i * HALF for i in (0, 2, 4, 6, 8, 9, 10))
TURN = 8
TO_RIGHT, TO_LEFT, TO_CROSS, TO_WRAP = 0, TURN, 2 * TURN, 2 * TURN + 2 * HALF
TO_RELAY, SENDS = TO_WRAP + HALF, TO_WRAP + 2 * HALF

NT = (((1,), (1,)), ((), ()))


def kernel(
    n, ints_ref, occ_in, vir_in, par_in, gamma,
    occ_ref, vir_ref, par_ref, own, nb, pbuf, xsend, xrecv, abuf, levcol, meta_own, meta_nb,
    send_sem, recv_sem, xs_sem, xr_sem, ms_sem, mr_sem, own_sem, in_sem,
):
    rows, aux = ints_ref.shape
    chunk = rows // PARTS
    step_rows = rows // 4
    virt = vir_ref.shape[1]
    me = lax.axis_index("occ")
    core = lax.axis_index("aux")
    x = me % RING
    right = me - x + (x + 1) % RING
    left = me - x + (x + RING - 1) % RING
    ymain = (me + n + RING - 2 * RING * (x // 2)) % n
    yback = (me + n - RING + 2 * RING * (x // 2)) % n
    near = ((me + 1) % n, (me + n - 1) % n, (me + 2) % n, (me + n - 2) % n)
    edge = (x == 0) | (x == RING - 1)

    first = 1 - (x + 3) // 4
    last = (x + 1) // 4

    def after(k):
        return (me + n - k) // n

    def before(k):
        return (2 * n - 1 - k - me) // n

    has_main = (1 - x // 2) * before(RING) + (x // 2) * after(RING)
    has_back = (1 - x // 2) * after(RING) + (x // 2) * before(RING)
    has_near = (before(1), after(1), before(2), after(2))
    edge_main = edge & (has_main == 1)
    edge_back = edge & (has_back == 1)

    def own_chunk(i):
        return ints_ref.at[pl.ds(pl.multiple_of(i * chunk, chunk), chunk)]

    def nb_chunk(i):
        return nb.at[pl.ds(pl.multiple_of(i * chunk, chunk), chunk)]

    def copy(src, to, ssem, device):
        return pltpu.make_async_remote_copy(
            src_ref=src, dst_ref=nb_chunk(to), send_sem=send_sem.at[ssem], recv_sem=recv_sem.at[to],
            device_id=(device, core), device_id_type=MESH,
        )

    def arrive(i):
        copy(nb_chunk(i), i, 0, right).wait_recv()

    def meta_copy(k, device):
        return pltpu.make_async_remote_copy(
            src_ref=meta_own, dst_ref=meta_nb.at[k], send_sem=ms_sem.at[k], recv_sem=mr_sem.at[k],
            device_id=(device, core), device_id_type=MESH,
        )

    def exchange(s):
        return pltpu.make_async_remote_copy(
            src_ref=xsend.at[s % 2], dst_ref=xrecv.at[s], send_sem=xs_sem.at[s], recv_sem=xr_sem.at[s],
            device_id=(me, 1 - core), device_id_type=MESH,
        )

    load = pltpu.make_async_copy(ints_ref, own, own_sem)
    load.start()
    small = [
        pltpu.make_async_copy(src, dst, in_sem.at[i])
        for i, (src, dst) in enumerate(((occ_in, occ_ref), (vir_in, vir_ref), (par_in, par_ref)))
    ]
    for item in small:
        item.start()

    barrier = pltpu.get_barrier_semaphore()
    def greet(device, other):
        pl.semaphore_signal(barrier, inc=1, device_id=(device, other), device_id_type=MESH)

    greet(right, core)
    greet(left, core)
    greet(me, 1 - core)
    for device, there in zip((ymain, yback, *near), (has_main, has_back, *has_near)):
        pl.when(there == 1)(functools.partial(greet, device, core))
    pl.semaphore_wait(barrier, 3 + has_main + has_back + sum(has_near))

    alternate = 2 * HALF - 3

    def on_own(k, act):
        @pl.when(k < 3)
        def _():
            act(k)

        @pl.when((k >= 3) & (k < alternate) & (k % 2 == 0))
        def _():
            act((k + 2) // 2)

    def on_passed(k, act):
        @pl.when((k >= 3) & (k < alternate) & (k % 2 == 1))
        def _():
            act((k - 3) // 2)

        @pl.when((k >= alternate) & (k < 2 * HALF))
        def _():
            act(k - HALF)

    def send_on_ring(k):
        turn = k % TURN

        def own_first(i):
            copy(own_chunk(i), LEFT + i, TO_RIGHT + turn, right).start()
            copy(own_chunk(HALF + i), RIGHT + HALF + i, TO_LEFT + turn, left).start()

        def passed(i):
            copy(nb_chunk(LEFT + i), FAR + i, TO_RIGHT + turn, right).start()
            copy(nb_chunk(RIGHT + HALF + i), FAR + HALF + i, TO_LEFT + turn, left).start()

        on_own(k, own_first)
        on_passed(k, passed)

        @pl.when((k >= 2 * HALF) & (k < TICKS))
        def _():
            i = k - 2 * HALF

            @pl.when(x < RING - 1)
            def _():
                copy(own_chunk(HALF + i), LEFT + HALF + i, TO_RIGHT + turn, right).start()

            @pl.when(x > 0)
            def _():
                copy(own_chunk(i), RIGHT + i, TO_LEFT + turn, left).start()

            @pl.when(edge_main)
            def _():
                arrive(RELAY + i)

            @pl.when((x == RING - 1) & (has_main == 1))
            def _():
                copy(nb_chunk(RELAY + i), LEFT + HALF + i, TO_RIGHT + turn, right).start()

            @pl.when((x == 0) & (has_main == 1))
            def _():
                copy(nb_chunk(RELAY + i), RIGHT + i, TO_LEFT + turn, left).start()

    pl.loop(0, AHEAD)(send_on_ring)

    @pl.when(edge_back)
    def _():
        @pl.loop(0, HALF)
        def _(i):
            copy(own_chunk(HALF * (x // 2) + i), RELAY + i, TO_RELAY + i, yback).start()

    for item in small:
        item.wait()
    for i in range(rows // virt):
        meta_own[0:1, i * virt : (i + 1) * virt] = vir_ref[...] - occ_ref[0:1, i : i + 1]
    for reach in (1, 2):
        found = [jnp.where(par_ref[0:1, i : i + 1] == me + reach, 1.0, 0.0) for i in range(2)]
        meta_own[reach : reach + 1, :] = jnp.broadcast_to(jnp.maximum(*found), (1, rows))
    meta_own[3:8, :] = jnp.zeros((5, rows), jnp.float32)
    for k, device in enumerate(near):
        pl.when(has_near[k] == 1)(meta_copy(k, device).start)
    levcol[...] = jnp.broadcast_to(meta_own[0:1, :], (levcol.shape[1], rows)).T

    @pl.loop(0, 4)
    def _(i):
        here = pl.ds(pl.multiple_of(i * step_rows, step_rows), step_rows)
        gamma[here] = jnp.zeros((step_rows, aux), jnp.float32)

    has_slot = (after(1), before(1), after(2), before(2))
    for k in range(4):

        @pl.when(has_slot[k] == 1)
        def _():
            meta_copy(k, right).wait_recv()
            listed = 1 + k // 2
            meta_nb[k, 3:4, :] = meta_own[listed : listed + 1, :] if k % 2 else meta_nb[k, listed : listed + 1, :]

    load.wait()

    def send_across(j):
        group = j // STEP
        i = HALF * (group % 2) + STEP * (group // 2) + j % STEP

        @pl.when(has_main == 1)
        def _():
            copy(nb_chunk(FAR + i), CROSS + i, TO_CROSS + j, ymain).start()

    def send_on_across(t):
        on_passed(t, send_across)

        @pl.when(t == 2 * HALF)
        def _():
            pl.loop(HALF, HALF + EARLY)(send_across)

        @pl.when((t >= 2 * HALF) & (t < TICKS - EARLY))
        def _():
            send_across(t - HALF + EARLY)

    def links(t):
        def own_first(i):
            arrive(LEFT + i)
            arrive(RIGHT + HALF + i)

            @pl.when(edge_main)
            def _():
                copy(nb_chunk((RIGHT + HALF) // 3 * x + i), WRAP + i, TO_WRAP + i, ymain).start()

        def passed(i):
            arrive(FAR + i)
            arrive(FAR + HALF + i)

        relayed = t // (2 * HALF)

        @pl.when((t < TICKS) & ((1 - has_main) * relayed * last == 0))
        def _():
            copy(nb_chunk(0), 0, TO_RIGHT + t % TURN, right).wait_send()

        @pl.when((t < TICKS) & ((1 - has_main) * relayed * first == 0))
        def _():
            copy(nb_chunk(0), 0, TO_LEFT + t % TURN, left).wait_send()

        @pl.when(t >= LATE)
        def _():
            on_own(t - LATE, own_first)
            on_passed(t - LATE, passed)

        send_on_ring(t + AHEAD)

        @pl.when(t >= LATE)
        def _():
            send_on_across(t - LATE)

    def ticks_before(s):
        return 8 + s + 3 * ((s + 11) // 16)

    def place(s):
        late = (s + 6) // 16
        early = 1 - late
        p = early * (s // 5) + late * ((s - 10) // 3)
        r = early * (s % 5) + late * (2 * ((s - 10) % 3))
        across = r // 4
        r2 = (r // 2) * (1 - across)
        h = r % 2
        base = (1 - across) * (1 - r2)
        swap = early * base * ((1 - h) * first + h * last)
        group = p + 2 * late
        at = (
            early * base * (1 - swap) * h * (RIGHT + HALF)
            + swap * WRAP
            + early * r2 * (FAR + HALF * h)
            + late * base * (LEFT + HALF)
            + late * r2 * RIGHT
            + (1 - across) * STEP * p
            + across * (CROSS + HALF * (group % 2) + STEP * (group // 2))
        )
        inside = (
            (1 - across) * (HALF * (early * h + late * base) + STEP * p)
            + across * (HALF * (group % 2) + STEP * (group // 2))
        )
        slot = early * (base * h + r2 * (3 - x // 2)) + late * r2 + across * (2 + x // 2)
        waits = swap + across + late * (1 - across)
        foreign = swap + across + late * (base * first + r2 * last)
        return at, inside, slot, waits, 1 - foreign * (1 - has_back)

    def block_rows(at):
        return pl.ds(pl.multiple_of(at * chunk, chunk), step_rows)

    m_rows = rows
    n_cols = aux

    def sent(s):
        @pl.when(place(s)[4] == 1)
        def _():
            exchange(s).wait_send()

    def products(s):
        at, _, _, waits, _ = place(s)

        @pl.when(waits == 1)
        def _():
            pl.loop(0, STEP)(lambda i: arrive(at + i))

        @pl.loop(0, rows // m_rows)
        def _(m):
            here = pl.ds(pl.multiple_of(m * m_rows, m_rows), m_rows)
            part = lax.dot_general(own[here], nb[block_rows(at)], NT, preferred_element_type=jnp.float32)
            pbuf[s % 2, here] = part
            xsend[s % 2, here] = part.astype(jnp.bfloat16)

        exchange(s).start()

    def finish(s):
        at, inside, slot, _, _ = place(s)
        exchange(s).wait_recv()
        cols = pl.ds(pl.multiple_of(inside * chunk, step_rows), step_rows)
        level = meta_nb[slot, 0:1, cols]
        live = meta_nb[slot, 3:4, cols]
        wide = step_rows // levcol.shape[1]

        @pl.loop(0, 4)
        def _(m):
            here = pl.ds(pl.multiple_of(m * step_rows, step_rows), step_rows)
            total = pbuf[s % 2, here] + xrecv[s, here].astype(jnp.float32)
            mine = levcol[here]
            mine = jnp.concatenate([mine] * wide, axis=1)
            abuf[here] = jnp.where(live > 0.5, total / (mine + level), 0.0).astype(jnp.bfloat16)

        @pl.loop(0, aux // n_cols)
        def _(c):
            there = pl.ds(pl.multiple_of(c * n_cols, n_cols), n_cols)
            gamma[:, there] += jnp.dot(abuf[...], nb[block_rows(at), there], preferred_element_type=jnp.float32)

    fine = PARTS // 16

    def links_until(start, end):
        @pl.loop(start, end)
        def _(t):
            @pl.when(t < TICKS + LATE)
            def _():
                links(t)

    links_until(0, fine * ticks_before(0))

    @pl.loop(0, STEPS + 2)
    def _(s):
        now = fine * ticks_before(s)
        made = s - (s + 2) // 16
        ended = s - 1 - (s + 1) // 16

        @pl.when((s != 13) & (made >= 2) & (made < STEPS))
        def _():
            sent(made - 2)

        @pl.when((s != 13) & (made < STEPS))
        def _():
            pl.when(place(made)[4] == 1)(functools.partial(products, made))

        links_until(now, now + 1)

        @pl.when((s != 14) & (ended >= 0))
        def _():
            pl.when(place(ended)[4] == 1)(functools.partial(finish, ended))

        links_until(now + 1, fine * ticks_before(s + 1))

    def sent_all(start, end):
        @pl.loop(start, end)
        def _(k):
            copy(nb_chunk(0), 0, k, right).wait_send()

    pl.when(has_main == 1)(functools.partial(sent_all, TO_CROSS, TO_WRAP))
    pl.when(edge_main)(functools.partial(sent_all, TO_WRAP, TO_RELAY))
    pl.when(edge_back)(functools.partial(sent_all, TO_RELAY, SENDS))
    for k in range(4):
        pl.when(has_near[k] == 1)(meta_copy(k, right).wait_send)
    sent(STEPS - 2)
    sent(STEPS - 1)


def body(n, ints, occ_energy, vir_energy, partners):
    _, rows, aux = ints.shape
    lanes = min(128, rows // 4)
    step_rows = rows // 4
    result = pl.pallas_call(
        functools.partial(kernel, n),
        out_shape=pltpu.VMEM((rows, aux), jnp.float32),
        in_specs=[
            pl.BlockSpec(memory_space=pl.ANY),
            pl.BlockSpec(memory_space=pl.ANY),
            pl.BlockSpec(memory_space=pl.ANY),
            pl.BlockSpec(memory_space=pl.ANY),
        ],
        out_specs=pl.BlockSpec(memory_space=pltpu.VMEM),
        scratch_shapes=[
            pltpu.VMEM(occ_energy.shape, jnp.float32),
            pltpu.VMEM(vir_energy.shape, jnp.float32),
            pltpu.VMEM(partners.shape, jnp.int32),
            pltpu.VMEM((rows, aux), jnp.bfloat16),
            pltpu.VMEM((CHUNKS * rows // PARTS, aux), jnp.bfloat16),
            pltpu.VMEM((2, rows, step_rows), jnp.float32),
            pltpu.VMEM((2, rows, step_rows), jnp.bfloat16),
            pltpu.VMEM((STEPS, rows, step_rows), jnp.bfloat16),
            pltpu.VMEM((rows, step_rows), jnp.bfloat16),
            pltpu.VMEM((rows, lanes), jnp.float32),
            pltpu.VMEM((8, rows), jnp.float32),
            pltpu.VMEM((4, 8, rows), jnp.float32),
            pltpu.SemaphoreType.DMA((SENDS,)),
            pltpu.SemaphoreType.DMA((CHUNKS,)),
            pltpu.SemaphoreType.DMA((STEPS,)),
            pltpu.SemaphoreType.DMA((STEPS,)),
            pltpu.SemaphoreType.DMA((4,)),
            pltpu.SemaphoreType.DMA((4,)),
            pltpu.SemaphoreType.DMA,
            pltpu.SemaphoreType.DMA((3,)),
        ],
        compiler_params=pltpu.CompilerParams(
            collective_id=0, has_side_effects=True, vmem_limit_bytes=55 * 2**20
        ),
        cost_estimate=pl.CostEstimate(
            flops=16 * rows * rows * aux, bytes_accessed=6 * rows * aux, transcendentals=0
        ),
    )(ints[0], occ_energy, vir_energy, partners)
    return result[None]


def solution(mesh):
    return jax.shard_map(
        functools.partial(body, mesh.shape["occ"]),
        mesh=mesh,
        in_specs=(P("occ", None, "aux"), P("occ", None), P("occ", None), P("occ", None)),
        out_specs=P("occ", None, "aux"),
        check_vma=False,
    )
```

```python
import functools

import jax
import jax.numpy as jnp
from jax import lax
from jax.experimental import pallas as pl
from jax.experimental.pallas import tpu as pltpu
from jax.sharding import PartitionSpec as P

MESH = pl.DeviceIdType.MESH
RING = 4
PARTS = 32
HALF = PARTS // 2
STEP = PARTS // 4
TICKS = 3 * HALF
AHEAD = 2
EARLY = 8
LATE = 1
STEPS = 16
LEFT, RIGHT, FAR, CROSS, WRAP, RELAY, CHUNKS = (i * HALF for i in (0, 2, 4, 6, 8, 9, 10))
TURN = 8
TO_RIGHT, TO_LEFT, TO_CROSS, TO_WRAP = 0, TURN, 2 * TURN, 2 * TURN + 2 * HALF
TO_RELAY, SENDS = TO_WRAP + HALF, TO_WRAP + 2 * HALF

NT = (((1,), (1,)), ((), ()))


def kernel(
    n, ints_ref, occ_in, vir_in, par_in, gamma,
    occ_ref, vir_ref, par_ref, own, nb, pbuf, xsend, xrecv, abuf, levcol, meta_own, meta_nb,
    send_sem, recv_sem, xs_sem, xr_sem, ms_sem, mr_sem, own_sem, in_sem,
):
    rows, aux = ints_ref.shape
    chunk = rows // PARTS
    step_rows = rows // 4
    virt = vir_ref.shape[1]
    me = lax.axis_index("occ")
    core = lax.axis_index("aux")
    x = me % RING
    right = me - x + (x + 1) % RING
    left = me - x + (x + RING - 1) % RING
    ymain = (me + n + RING - 2 * RING * (x // 2)) % n
    yback = (me + n - RING + 2 * RING * (x // 2)) % n
    near = ((me + 1) % n, (me + n - 1) % n, (me + 2) % n, (me + n - 2) % n)
    edge = (x == 0) | (x == RING - 1)

    first = 1 - (x + 3) // 4
    last = (x + 1) // 4

    def after(k):
        return (me + n - k) // n

    def before(k):
        return (2 * n - 1 - k - me) // n

    has_main = (1 - x // 2) * before(RING) + (x // 2) * after(RING)
    has_back = (1 - x // 2) * after(RING) + (x // 2) * before(RING)
    has_near = (before(1), after(1), before(2), after(2))
    edge_main = edge & (has_main == 1)
    edge_back = edge & (has_back == 1)

    def own_chunk(i):
        return ints_ref.at[pl.ds(pl.multiple_of(i * chunk, chunk), chunk)]

    def nb_chunk(i):
        return nb.at[pl.ds(pl.multiple_of(i * chunk, chunk), chunk)]

    def copy(src, to, ssem, device):
        return pltpu.make_async_remote_copy(
            src_ref=src, dst_ref=nb_chunk(to), send_sem=send_sem.at[ssem], recv_sem=recv_sem.at[to],
            device_id=(device, core), device_id_type=MESH,
        )

    def arrive(i):
        copy(nb_chunk(i), i, 0, right).wait_recv()

    def meta_copy(k, device):
        return pltpu.make_async_remote_copy(
            src_ref=meta_own, dst_ref=meta_nb.at[k], send_sem=ms_sem.at[k], recv_sem=mr_sem.at[k],
            device_id=(device, core), device_id_type=MESH,
        )

    def exchange(s):
        return pltpu.make_async_remote_copy(
            src_ref=xsend.at[s % 2], dst_ref=xrecv.at[s], send_sem=xs_sem.at[s], recv_sem=xr_sem.at[s],
            device_id=(me, 1 - core), device_id_type=MESH,
        )

    load = pltpu.make_async_copy(ints_ref, own, own_sem)
    load.start()
    small = [
        pltpu.make_async_copy(src, dst, in_sem.at[i])
        for i, (src, dst) in enumerate(((occ_in, occ_ref), (vir_in, vir_ref), (par_in, par_ref)))
    ]
    for item in small:
        item.start()

    barrier = pltpu.get_barrier_semaphore()
    def greet(device, other):
        pl.semaphore_signal(barrier, inc=1, device_id=(device, other), device_id_type=MESH)

    greet(right, core)
    greet(left, core)
    greet(me, 1 - core)
    for device, there in zip((ymain, yback, *near), (has_main, has_back, *has_near)):
        pl.when(there == 1)(functools.partial(greet, device, core))
    pl.semaphore_wait(barrier, 3 + has_main + has_back + sum(has_near))

    alternate = 2 * HALF - 3

    def on_own(k, act):
        @pl.when(k < 3)
        def _():
            act(k)

        @pl.when((k >= 3) & (k < alternate) & (k % 2 == 0))
        def _():
            act((k + 2) // 2)

    def on_passed(k, act):
        @pl.when((k >= 3) & (k < alternate) & (k % 2 == 1))
        def _():
            act((k - 3) // 2)

        @pl.when((k >= alternate) & (k < 2 * HALF))
        def _():
            act(k - HALF)

    def send_on_ring(k):
        turn = k % TURN

        def own_first(i):
            copy(own_chunk(i), LEFT + i, TO_RIGHT + turn, right).start()
            copy(own_chunk(HALF + i), RIGHT + HALF + i, TO_LEFT + turn, left).start()

        def passed(i):
            copy(nb_chunk(LEFT + i), FAR + i, TO_RIGHT + turn, right).start()
            copy(nb_chunk(RIGHT + HALF + i), FAR + HALF + i, TO_LEFT + turn, left).start()

        on_own(k, own_first)
        on_passed(k, passed)

        @pl.when((k >= 2 * HALF) & (k < TICKS))
        def _():
            i = k - 2 * HALF

            @pl.when(x < RING - 1)
            def _():
                copy(own_chunk(HALF + i), LEFT + HALF + i, TO_RIGHT + turn, right).start()

            @pl.when(x > 0)
            def _():
                copy(own_chunk(i), RIGHT + i, TO_LEFT + turn, left).start()

            @pl.when(edge_main)
            def _():
                arrive(RELAY + i)

            @pl.when((x == RING - 1) & (has_main == 1))
            def _():
                copy(nb_chunk(RELAY + i), LEFT + HALF + i, TO_RIGHT + turn, right).start()

            @pl.when((x == 0) & (has_main == 1))
            def _():
                copy(nb_chunk(RELAY + i), RIGHT + i, TO_LEFT + turn, left).start()

    pl.loop(0, AHEAD)(send_on_ring)

    @pl.when(edge_back)
    def _():
        @pl.loop(0, HALF)
        def _(i):
            copy(own_chunk(HALF * (x // 2) + i), RELAY + i, TO_RELAY + i, yback).start()

    for item in small:
        item.wait()
    for i in range(rows // virt):
        meta_own[0:1, i * virt : (i + 1) * virt] = vir_ref[...] - occ_ref[0:1, i : i + 1]
    for reach in (1, 2):
        found = [jnp.where(par_ref[0:1, i : i + 1] == me + reach, 1.0, 0.0) for i in range(2)]
        meta_own[reach : reach + 1, :] = jnp.broadcast_to(jnp.maximum(*found), (1, rows))
    meta_own[3:8, :] = jnp.zeros((5, rows), jnp.float32)
    for k, device in enumerate(near):
        pl.when(has_near[k] == 1)(meta_copy(k, device).start)
    levcol[...] = jnp.broadcast_to(meta_own[0:1, :], (levcol.shape[1], rows)).T

    @pl.loop(0, 4)
    def _(i):
        here = pl.ds(pl.multiple_of(i * step_rows, step_rows), step_rows)
        gamma[here] = jnp.zeros((step_rows, aux), jnp.float32)

    has_slot = (after(1), before(1), after(2), before(2))
    for k in range(4):

        @pl.when(has_slot[k] == 1)
        def _():
            meta_copy(k, right).wait_recv()
            listed = 1 + k // 2
            meta_nb[k, 3:4, :] = meta_own[listed : listed + 1, :] if k % 2 else meta_nb[k, listed : listed + 1, :]

    load.wait()

    def send_across(j):
        group = j // STEP
        i = HALF * (group % 2) + STEP * (group // 2) + j % STEP

        @pl.when(has_main == 1)
        def _():
            copy(nb_chunk(FAR + i), CROSS + i, TO_CROSS + j, ymain).start()

    def send_on_across(t):
        on_passed(t, send_across)

        @pl.when(t == 2 * HALF)
        def _():
            pl.loop(HALF, HALF + EARLY)(send_across)

        @pl.when((t >= 2 * HALF) & (t < TICKS - EARLY))
        def _():
            send_across(t - HALF + EARLY)

    def links(t):
        def own_first(i):
            arrive(LEFT + i)
            arrive(RIGHT + HALF + i)

            @pl.when(edge_main)
            def _():
                copy(nb_chunk((RIGHT + HALF) // 3 * x + i), WRAP + i, TO_WRAP + i, ymain).start()

        def passed(i):
            arrive(FAR + i)
            arrive(FAR + HALF + i)

        relayed = t // (2 * HALF)

        @pl.when((t < TICKS) & ((1 - has_main) * relayed * last == 0))
        def _():
            copy(nb_chunk(0), 0, TO_RIGHT + t % TURN, right).wait_send()

        @pl.when((t < TICKS) & ((1 - has_main) * relayed * first == 0))
        def _():
            copy(nb_chunk(0), 0, TO_LEFT + t % TURN, left).wait_send()

        @pl.when(t >= LATE)
        def _():
            on_own(t - LATE, own_first)
            on_passed(t - LATE, passed)

        send_on_ring(t + AHEAD)

        @pl.when(t >= LATE)
        def _():
            send_on_across(t - LATE)

    def ticks_before(s):
        return 8 + s + 3 * ((s + 11) // 16)

    def place(s):
        late = (s + 6) // 16
        early = 1 - late
        p = early * (s // 5) + late * ((s - 10) // 3)
        r = early * (s % 5) + late * (2 * ((s - 10) % 3))
        across = r // 4
        r2 = (r // 2) * (1 - across)
        h = r % 2
        base = (1 - across) * (1 - r2)
        swap = early * base * ((1 - h) * first + h * last)
        group = p + 2 * late
        at = (
            early * base * (1 - swap) * h * (RIGHT + HALF)
            + swap * WRAP
            + early * r2 * (FAR + HALF * h)
            + late * base * (LEFT + HALF)
            + late * r2 * RIGHT
            + (1 - across) * STEP * p
            + across * (CROSS + HALF * (group % 2) + STEP * (group // 2))
        )
        inside = (
            (1 - across) * (HALF * (early * h + late * base) + STEP * p)
            + across * (HALF * (group % 2) + STEP * (group // 2))
        )
        slot = early * (base * h + r2 * (3 - x // 2)) + late * r2 + across * (2 + x // 2)
        waits = swap + across + late * (1 - across)
        foreign = swap + across + late * (base * first + r2 * last)
        return at, inside, slot, waits, 1 - foreign * (1 - has_back)

    def block_rows(at):
        return pl.ds(pl.multiple_of(at * chunk, chunk), step_rows)

    m_rows = rows
    n_cols = aux

    def sent(s):
        @pl.when(place(s)[4] == 1)
        def _():
            exchange(s).wait_send()

    def products(s):
        at, _, _, waits, _ = place(s)

        @pl.when(waits == 1)
        def _():
            pl.loop(0, STEP)(lambda i: arrive(at + i))

        @pl.loop(0, rows // m_rows)
        def _(m):
            here = pl.ds(pl.multiple_of(m * m_rows, m_rows), m_rows)
            part = lax.dot_general(own[here], nb[block_rows(at)], NT, preferred_element_type=jnp.float32)
            pbuf[s % 2, here] = part
            xsend[s % 2, here] = part.astype(jnp.bfloat16)

        exchange(s).start()

    def finish(s):
        at, inside, slot, _, _ = place(s)
        exchange(s).wait_recv()
        cols = pl.ds(pl.multiple_of(inside * chunk, step_rows), step_rows)
        level = meta_nb[slot, 0:1, cols]
        live = meta_nb[slot, 3:4, cols]
        wide = step_rows // levcol.shape[1]

        @pl.loop(0, 1)
        def _(m):
            here = pl.ds(pl.multiple_of(m * rows, rows), rows)
            total = pbuf[s % 2, here] + xrecv[s, here].astype(jnp.float32)
            mine = levcol[here]
            mine = jnp.concatenate([mine] * wide, axis=1)
            abuf[here] = jnp.where(live > 0.5, total / (mine + level), 0.0).astype(jnp.bfloat16)

        @pl.loop(0, aux // n_cols)
        def _(c):
            there = pl.ds(pl.multiple_of(c * n_cols, n_cols), n_cols)
            gamma[:, there] += jnp.dot(abuf[...], nb[block_rows(at), there], preferred_element_type=jnp.float32)

    fine = PARTS // 16

    def links_until(start, end):
        @pl.loop(start, end)
        def _(t):
            @pl.when(t < TICKS + LATE)
            def _():
                links(t)

    links_until(0, fine * ticks_before(0))

    @pl.loop(0, STEPS + 2)
    def _(s):
        now = fine * ticks_before(s)
        made = s - (s + 2) // 16
        ended = s - 1 - (s + 1) // 16

        @pl.when((s != 13) & (made >= 2) & (made < STEPS))
        def _():
            sent(made - 2)

        @pl.when((s != 13) & (made < STEPS))
        def _():
            pl.when(place(made)[4] == 1)(functools.partial(products, made))

        links_until(now, now + 1)

        @pl.when((s != 14) & (ended >= 0))
        def _():
            pl.when(place(ended)[4] == 1)(functools.partial(finish, ended))

        links_until(now + 1, fine * ticks_before(s + 1))

    def sent_all(start, end):
        @pl.loop(start, end)
        def _(k):
            copy(nb_chunk(0), 0, k, right).wait_send()

    pl.when(has_main == 1)(functools.partial(sent_all, TO_CROSS, TO_WRAP))
    pl.when(edge_main)(functools.partial(sent_all, TO_WRAP, TO_RELAY))
    pl.when(edge_back)(functools.partial(sent_all, TO_RELAY, SENDS))
    for k in range(4):
        pl.when(has_near[k] == 1)(meta_copy(k, right).wait_send)
    sent(STEPS - 2)
    sent(STEPS - 1)


def body(n, ints, occ_energy, vir_energy, partners):
    _, rows, aux = ints.shape
    lanes = min(128, rows // 4)
    step_rows = rows // 4
    result = pl.pallas_call(
        functools.partial(kernel, n),
        out_shape=pltpu.VMEM((rows, aux), jnp.float32),
        in_specs=[
            pl.BlockSpec(memory_space=pl.ANY),
            pl.BlockSpec(memory_space=pl.ANY),
            pl.BlockSpec(memory_space=pl.ANY),
            pl.BlockSpec(memory_space=pl.ANY),
        ],
        out_specs=pl.BlockSpec(memory_space=pltpu.VMEM),
        scratch_shapes=[
            pltpu.VMEM(occ_energy.shape, jnp.float32),
            pltpu.VMEM(vir_energy.shape, jnp.float32),
            pltpu.VMEM(partners.shape, jnp.int32),
            pltpu.VMEM((rows, aux), jnp.bfloat16),
            pltpu.VMEM((CHUNKS * rows // PARTS, aux), jnp.bfloat16),
            pltpu.VMEM((2, rows, step_rows), jnp.float32),
            pltpu.VMEM((2, rows, step_rows), jnp.bfloat16),
            pltpu.VMEM((STEPS, rows, step_rows), jnp.bfloat16),
            pltpu.VMEM((rows, step_rows), jnp.bfloat16),
            pltpu.VMEM((rows, lanes), jnp.float32),
            pltpu.VMEM((8, rows), jnp.float32),
            pltpu.VMEM((4, 8, rows), jnp.float32),
            pltpu.SemaphoreType.DMA((SENDS,)),
            pltpu.SemaphoreType.DMA((CHUNKS,)),
            pltpu.SemaphoreType.DMA((STEPS,)),
            pltpu.SemaphoreType.DMA((STEPS,)),
            pltpu.SemaphoreType.DMA((4,)),
            pltpu.SemaphoreType.DMA((4,)),
            pltpu.SemaphoreType.DMA,
            pltpu.SemaphoreType.DMA((3,)),
        ],
        compiler_params=pltpu.CompilerParams(
            collective_id=0, has_side_effects=True, vmem_limit_bytes=55 * 2**20
        ),
        cost_estimate=pl.CostEstimate(
            flops=16 * rows * rows * aux, bytes_accessed=6 * rows * aux, transcendentals=0
        ),
    )(ints[0], occ_energy, vir_energy, partners)
    return result[None]


def solution(mesh):
    return jax.shard_map(
        functools.partial(body, mesh.shape["occ"]),
        mesh=mesh,
        in_specs=(P("occ", None, "aux"), P("occ", None), P("occ", None), P("occ", None)),
        out_specs=P("occ", None, "aux"),
        check_vma=False,
    )
```

```python
import functools

import jax
import jax.numpy as jnp
from jax import lax
from jax.experimental import pallas as pl
from jax.experimental.pallas import tpu as pltpu
from jax.sharding import PartitionSpec as P

MESH = pl.DeviceIdType.MESH
RING = 4
PARTS = 32
HALF = PARTS // 2
STEP = PARTS // 4
TICKS = 3 * HALF
AHEAD = 2
EARLY = 12
LATE = 1
STEPS = 16
LEFT, RIGHT, FAR, CROSS, WRAP, RELAY, CHUNKS = (i * HALF for i in (0, 2, 4, 6, 8, 9, 10))
TURN = 8
TO_RIGHT, TO_LEFT, TO_CROSS, TO_WRAP = 0, TURN, 2 * TURN, 2 * TURN + 2 * HALF
TO_RELAY, SENDS = TO_WRAP + HALF, TO_WRAP + 2 * HALF

NT = (((1,), (1,)), ((), ()))


def kernel(
    n, ints_ref, occ_in, vir_in, par_in, gamma,
    occ_ref, vir_ref, par_ref, own, nb, pbuf, xsend, xrecv, abuf, levcol, meta_own, meta_nb,
    send_sem, recv_sem, xs_sem, xr_sem, ms_sem, mr_sem, own_sem, in_sem,
):
    rows, aux = ints_ref.shape
    chunk = rows // PARTS
    step_rows = rows // 4
    virt = vir_ref.shape[1]
    me = lax.axis_index("occ")
    core = lax.axis_index("aux")
    x = me % RING
    right = me - x + (x + 1) % RING
    left = me - x + (x + RING - 1) % RING
    ymain = (me + n + RING - 2 * RING * (x // 2)) % n
    yback = (me + n - RING + 2 * RING * (x // 2)) % n
    near = ((me + 1) % n, (me + n - 1) % n, (me + 2) % n, (me + n - 2) % n)
    edge = (x == 0) | (x == RING - 1)

    first = 1 - (x + 3) // 4
    last = (x + 1) // 4

    def after(k):
        return (me + n - k) // n

    def before(k):
        return (2 * n - 1 - k - me) // n

    has_main = (1 - x // 2) * before(RING) + (x // 2) * after(RING)
    has_back = (1 - x // 2) * after(RING) + (x // 2) * before(RING)
    has_near = (before(1), after(1), before(2), after(2))
    edge_main = edge & (has_main == 1)
    edge_back = edge & (has_back == 1)

    def own_chunk(i):
        return ints_ref.at[pl.ds(pl.multiple_of(i * chunk, chunk), chunk)]

    def nb_chunk(i):
        return nb.at[pl.ds(pl.multiple_of(i * chunk, chunk), chunk)]

    def copy(src, to, ssem, device):
        return pltpu.make_async_remote_copy(
            src_ref=src, dst_ref=nb_chunk(to), send_sem=send_sem.at[ssem], recv_sem=recv_sem.at[to],
            device_id=(device, core), device_id_type=MESH,
        )

    def arrive(i):
        copy(nb_chunk(i), i, 0, right).wait_recv()

    def meta_copy(k, device):
        return pltpu.make_async_remote_copy(
            src_ref=meta_own, dst_ref=meta_nb.at[k], send_sem=ms_sem.at[k], recv_sem=mr_sem.at[k],
            device_id=(device, core), device_id_type=MESH,
        )

    def exchange(s):
        return pltpu.make_async_remote_copy(
            src_ref=xsend.at[s % 2], dst_ref=xrecv.at[s], send_sem=xs_sem.at[s], recv_sem=xr_sem.at[s],
            device_id=(me, 1 - core), device_id_type=MESH,
        )

    load = pltpu.make_async_copy(ints_ref, own, own_sem)
    load.start()
    small = [
        pltpu.make_async_copy(src, dst, in_sem.at[i])
        for i, (src, dst) in enumerate(((occ_in, occ_ref), (vir_in, vir_ref), (par_in, par_ref)))
    ]
    for item in small:
        item.start()

    barrier = pltpu.get_barrier_semaphore()
    def greet(device, other):
        pl.semaphore_signal(barrier, inc=1, device_id=(device, other), device_id_type=MESH)

    greet(right, core)
    greet(left, core)
    greet(me, 1 - core)
    for device, there in zip((ymain, yback, *near), (has_main, has_back, *has_near)):
        pl.when(there == 1)(functools.partial(greet, device, core))
    pl.semaphore_wait(barrier, 3 + has_main + has_back + sum(has_near))

    alternate = 2 * HALF - 3

    def on_own(k, act):
        @pl.when(k < 3)
        def _():
            act(k)

        @pl.when((k >= 3) & (k < alternate) & (k % 2 == 0))
        def _():
            act((k + 2) // 2)

    def on_passed(k, act):
        @pl.when((k >= 3) & (k < alternate) & (k % 2 == 1))
        def _():
            act((k - 3) // 2)

        @pl.when((k >= alternate) & (k < 2 * HALF))
        def _():
            act(k - HALF)

    def send_on_ring(k):
        turn = k % TURN

        def own_first(i):
            copy(own_chunk(i), LEFT + i, TO_RIGHT + turn, right).start()
            copy(own_chunk(HALF + i), RIGHT + HALF + i, TO_LEFT + turn, left).start()

        def passed(i):
            copy(nb_chunk(LEFT + i), FAR + i, TO_RIGHT + turn, right).start()
            copy(nb_chunk(RIGHT + HALF + i), FAR + HALF + i, TO_LEFT + turn, left).start()

        on_own(k, own_first)
        on_passed(k, passed)

        @pl.when((k >= 2 * HALF) & (k < TICKS))
        def _():
            i = k - 2 * HALF

            @pl.when(x < RING - 1)
            def _():
                copy(own_chunk(HALF + i), LEFT + HALF + i, TO_RIGHT + turn, right).start()

            @pl.when(x > 0)
            def _():
                copy(own_chunk(i), RIGHT + i, TO_LEFT + turn, left).start()

            @pl.when(edge_main)
            def _():
                arrive(RELAY + i)

            @pl.when((x == RING - 1) & (has_main == 1))
            def _():
                copy(nb_chunk(RELAY + i), LEFT + HALF + i, TO_RIGHT + turn, right).start()

            @pl.when((x == 0) & (has_main == 1))
            def _():
                copy(nb_chunk(RELAY + i), RIGHT + i, TO_LEFT + turn, left).start()

    pl.loop(0, AHEAD)(send_on_ring)

    @pl.when(edge_back)
    def _():
        @pl.loop(0, HALF)
        def _(i):
            copy(own_chunk(HALF * (x // 2) + i), RELAY + i, TO_RELAY + i, yback).start()

    for item in small:
        item.wait()
    for i in range(rows // virt):
        meta_own[0:1, i * virt : (i + 1) * virt] = vir_ref[...] - occ_ref[0:1, i : i + 1]
    for reach in (1, 2):
        found = [jnp.where(par_ref[0:1, i : i + 1] == me + reach, 1.0, 0.0) for i in range(2)]
        meta_own[reach : reach + 1, :] = jnp.broadcast_to(jnp.maximum(*found), (1, rows))
    meta_own[3:8, :] = jnp.zeros((5, rows), jnp.float32)
    for k, device in enumerate(near):
        pl.when(has_near[k] == 1)(meta_copy(k, device).start)
    levcol[...] = jnp.broadcast_to(meta_own[0:1, :], (levcol.shape[1], rows)).T

    @pl.loop(0, 4)
    def _(i):
        here = pl.ds(pl.multiple_of(i * step_rows, step_rows), step_rows)
        gamma[here] = jnp.zeros((step_rows, aux), jnp.float32)

    has_slot = (after(1), before(1), after(2), before(2))
    for k in range(4):

        @pl.when(has_slot[k] == 1)
        def _():
            meta_copy(k, right).wait_recv()
            listed = 1 + k // 2
            meta_nb[k, 3:4, :] = meta_own[listed : listed + 1, :] if k % 2 else meta_nb[k, listed : listed + 1, :]

    load.wait()

    def send_across(j):
        group = j // STEP
        i = HALF * (group % 2) + STEP * (group // 2) + j % STEP

        @pl.when(has_main == 1)
        def _():
            copy(nb_chunk(FAR + i), CROSS + i, TO_CROSS + j, ymain).start()

    def send_on_across(t):
        on_passed(t, send_across)

        @pl.when(t == 2 * HALF)
        def _():
            pl.loop(HALF, HALF + EARLY)(send_across)

        @pl.when((t >= 2 * HALF) & (t < TICKS - EARLY))
        def _():
            send_across(t - HALF + EARLY)

    def links(t):
        def own_first(i):
            arrive(LEFT + i)
            arrive(RIGHT + HALF + i)

            @pl.when(edge_main)
            def _():
                copy(nb_chunk((RIGHT + HALF) // 3 * x + i), WRAP + i, TO_WRAP + i, ymain).start()

        def passed(i):
            arrive(FAR + i)
            arrive(FAR + HALF + i)

        relayed = t // (2 * HALF)

        @pl.when((t < TICKS) & ((1 - has_main) * relayed * last == 0))
        def _():
            copy(nb_chunk(0), 0, TO_RIGHT + t % TURN, right).wait_send()

        @pl.when((t < TICKS) & ((1 - has_main) * relayed * first == 0))
        def _():
            copy(nb_chunk(0), 0, TO_LEFT + t % TURN, left).wait_send()

        @pl.when(t >= LATE)
        def _():
            on_own(t - LATE, own_first)
            on_passed(t - LATE, passed)

        send_on_ring(t + AHEAD)

        @pl.when(t >= LATE)
        def _():
            send_on_across(t - LATE)

    def ticks_before(s):
        return 8 + s + 3 * ((s + 11) // 16)

    def place(s):
        late = (s + 6) // 16
        early = 1 - late
        p = early * (s // 5) + late * ((s - 10) // 3)
        r = early * (s % 5) + late * (2 * ((s - 10) % 3))
        across = r // 4
        r2 = (r // 2) * (1 - across)
        h = r % 2
        base = (1 - across) * (1 - r2)
        swap = early * base * ((1 - h) * first + h * last)
        group = p + 2 * late
        at = (
            early * base * (1 - swap) * h * (RIGHT + HALF)
            + swap * WRAP
            + early * r2 * (FAR + HALF * h)
            + late * base * (LEFT + HALF)
            + late * r2 * RIGHT
            + (1 - across) * STEP * p
            + across * (CROSS + HALF * (group % 2) + STEP * (group // 2))
        )
        inside = (
            (1 - across) * (HALF * (early * h + late * base) + STEP * p)
            + across * (HALF * (group % 2) + STEP * (group // 2))
        )
        slot = early * (base * h + r2 * (3 - x // 2)) + late * r2 + across * (2 + x // 2)
        waits = swap + across + late * (1 - across)
        foreign = swap + across + late * (base * first + r2 * last)
        return at, inside, slot, waits, 1 - foreign * (1 - has_back)

    def block_rows(at):
        return pl.ds(pl.multiple_of(at * chunk, chunk), step_rows)

    m_rows = rows
    n_cols = aux

    def sent(s):
        @pl.when(place(s)[4] == 1)
        def _():
            exchange(s).wait_send()

    def products(s):
        at, _, _, waits, _ = place(s)

        @pl.when(waits == 1)
        def _():
            pl.loop(0, STEP)(lambda i: arrive(at + i))

        @pl.loop(0, rows // m_rows)
        def _(m):
            here = pl.ds(pl.multiple_of(m * m_rows, m_rows), m_rows)
            part = lax.dot_general(own[here], nb[block_rows(at)], NT, preferred_element_type=jnp.float32)
            pbuf[s % 2, here] = part
            xsend[s % 2, here] = part.astype(jnp.bfloat16)

        exchange(s).start()

    def finish(s):
        at, inside, slot, _, _ = place(s)
        exchange(s).wait_recv()
        cols = pl.ds(pl.multiple_of(inside * chunk, step_rows), step_rows)
        level = meta_nb[slot, 0:1, cols]
        live = meta_nb[slot, 3:4, cols]
        wide = step_rows // levcol.shape[1]

        @pl.loop(0, 1)
        def _(m):
            here = pl.ds(pl.multiple_of(m * rows, rows), rows)
            total = pbuf[s % 2, here] + xrecv[s, here].astype(jnp.float32)
            mine = levcol[here]
            mine = jnp.concatenate([mine] * wide, axis=1)
            abuf[here] = jnp.where(live > 0.5, total / (mine + level), 0.0).astype(jnp.bfloat16)

        @pl.loop(0, aux // n_cols)
        def _(c):
            there = pl.ds(pl.multiple_of(c * n_cols, n_cols), n_cols)
            gamma[:, there] += jnp.dot(abuf[...], nb[block_rows(at), there], preferred_element_type=jnp.float32)

    fine = PARTS // 16

    def links_until(start, end):
        @pl.loop(start, end)
        def _(t):
            @pl.when(t < TICKS + LATE)
            def _():
                links(t)

    links_until(0, fine * ticks_before(0))

    @pl.loop(0, STEPS + 2)
    def _(s):
        now = fine * ticks_before(s)
        made = s - (s + 2) // 16
        ended = s - 1 - (s + 1) // 16

        @pl.when((s != 13) & (made >= 2) & (made < STEPS))
        def _():
            sent(made - 2)

        @pl.when((s != 13) & (made < STEPS))
        def _():
            pl.when(place(made)[4] == 1)(functools.partial(products, made))

        links_until(now, now + 1)

        @pl.when((s != 14) & (ended >= 0))
        def _():
            pl.when(place(ended)[4] == 1)(functools.partial(finish, ended))

        links_until(now + 1, fine * ticks_before(s + 1))

    def sent_all(start, end):
        @pl.loop(start, end)
        def _(k):
            copy(nb_chunk(0), 0, k, right).wait_send()

    pl.when(has_main == 1)(functools.partial(sent_all, TO_CROSS, TO_WRAP))
    pl.when(edge_main)(functools.partial(sent_all, TO_WRAP, TO_RELAY))
    pl.when(edge_back)(functools.partial(sent_all, TO_RELAY, SENDS))
    for k in range(4):
        pl.when(has_near[k] == 1)(meta_copy(k, right).wait_send)
    sent(STEPS - 2)
    sent(STEPS - 1)


def body(n, ints, occ_energy, vir_energy, partners):
    _, rows, aux = ints.shape
    lanes = min(128, rows // 4)
    step_rows = rows // 4
    result = pl.pallas_call(
        functools.partial(kernel, n),
        out_shape=pltpu.VMEM((rows, aux), jnp.float32),
        in_specs=[
            pl.BlockSpec(memory_space=pl.ANY),
            pl.BlockSpec(memory_space=pl.ANY),
            pl.BlockSpec(memory_space=pl.ANY),
            pl.BlockSpec(memory_space=pl.ANY),
        ],
        out_specs=pl.BlockSpec(memory_space=pltpu.VMEM),
        scratch_shapes=[
            pltpu.VMEM(occ_energy.shape, jnp.float32),
            pltpu.VMEM(vir_energy.shape, jnp.float32),
            pltpu.VMEM(partners.shape, jnp.int32),
            pltpu.VMEM((rows, aux), jnp.bfloat16),
            pltpu.VMEM((CHUNKS * rows // PARTS, aux), jnp.bfloat16),
            pltpu.VMEM((2, rows, step_rows), jnp.float32),
            pltpu.VMEM((2, rows, step_rows), jnp.bfloat16),
            pltpu.VMEM((STEPS, rows, step_rows), jnp.bfloat16),
            pltpu.VMEM((rows, step_rows), jnp.bfloat16),
            pltpu.VMEM((rows, lanes), jnp.float32),
            pltpu.VMEM((8, rows), jnp.float32),
            pltpu.VMEM((4, 8, rows), jnp.float32),
            pltpu.SemaphoreType.DMA((SENDS,)),
            pltpu.SemaphoreType.DMA((CHUNKS,)),
            pltpu.SemaphoreType.DMA((STEPS,)),
            pltpu.SemaphoreType.DMA((STEPS,)),
            pltpu.SemaphoreType.DMA((4,)),
            pltpu.SemaphoreType.DMA((4,)),
            pltpu.SemaphoreType.DMA,
            pltpu.SemaphoreType.DMA((3,)),
        ],
        compiler_params=pltpu.CompilerParams(
            collective_id=0, has_side_effects=True, vmem_limit_bytes=55 * 2**20
        ),
        cost_estimate=pl.CostEstimate(
            flops=16 * rows * rows * aux, bytes_accessed=6 * rows * aux, transcendentals=0
        ),
    )(ints[0], occ_energy, vir_energy, partners)
    return result[None]


def solution(mesh):
    return jax.shard_map(
        functools.partial(body, mesh.shape["occ"]),
        mesh=mesh,
        in_specs=(P("occ", None, "aux"), P("occ", None), P("occ", None), P("occ", None)),
        out_specs=P("occ", None, "aux"),
        check_vma=False,
    )
```
